32 devices in a mesh: slab: 2 (over x), brick: 16 (over z, y, core).
Axes of the slice: x: 2, y: 2, z: 4, core: 2. Of those that a mesh axis runs over, the one named last changes fastest.
Arguments:
- features: bfloat16 [64, 64, 512], P(('slab', 'brick')), may hold values from -6 to 6
- weight: bfloat16 [27, 64, 64], replicated, may hold values from -0.15625 to 0.15625
- cotangent: bfloat16 [64, 64, 512], P(('slab', 'brick')), may hold values from -6 to 6
- occupancy: int32 [64, 24], P(('slab', 'brick')), may hold values from 0 to 4194303, as said below
- neighbours: int32 [64, 27], P(('slab', 'brick')), may hold values from -1 to 63, as said below
Outputs:
- output: bfloat16 [64, 64, 512], P(('slab', 'brick'))
- grad_input: bfloat16 [64, 64, 512], P(('slab', 'brick'))
- grad_weight: float32 [27, 64, 64], replicated
The draws below stay inside these ranges and needn't reach their ends.
Inputs may be any that keep to these rules, and one draw needn't show every extreme that they name: `neighbours`: slot j of the device at (slab s, brick t), that is slot (16 s + t) * 2 + j, holds the brick of z layer 2 s + j and column t along x, at some row y; slot 0 of every device holds a brick, the others may be absent. For offset k = 9 (a + 1) + 3 (c + 1) + (e + 1), the entry of a present slot is the slot that holds the brick at layer 2 s + j + a, row y + c, column t + e if that brick is present, else -1; an absent slot's entries are all -1. The lists are symmetric, and the middle entry of a present slot is the slot itself. Bit j of word w of a slot is the occupancy of voxel 22 w + j; bits from voxel 512 on are zero. Absent slots are wholly unoccupied; slot 0 is fully occupied.
All inputs are finite; a program needn't handle non-finite values.
Results may differ from the reference program's by a relative error of at most 0.001.
Values may be sent and summed in bfloat16 or wider, within the bound.
A program may use at most 64 MiB of HBM per device.

```python
import math
import jax
import jax.numpy as jnp
from jax import lax

C = 64
EDGE = 8
TAPS = 27
ZPS = 2
YB = 64
VOX = 512
WORDS = 24
LAYERS = 2
COLUMNS = 16
SLOTS = 64


def brick_layout(key):
    base = jax.random.fold_in(key, 11)
    keys = jax.random.split(base, 4)
    steps = jax.random.randint(keys[0], (COLUMNS,), -1, 2)
    start = jax.random.randint(keys[1], (), 0, YB - 1)
    walk = jnp.clip(start + jnp.cumsum(steps).astype(jnp.int32), 0, YB - 2).astype(jnp.int32)
    lift = jax.random.randint(keys[2], (LAYERS, ZPS), 0, 2)
    lift = lift.at[:, 0].set(0)
    present = jax.random.randint(keys[3], (LAYERS, COLUMNS, ZPS), 0, 2) == 1
    present = present.at[:, :, 0].set(True)
    present = present.at[LAYERS - 1, COLUMNS - 1, ZPS - 1].set(True)
    rows = walk[None, :, None] + lift[:, None, :]
    return (present, rows)


def draw_neighbours(key, part):
    present, rows = brick_layout(key)
    offset = jnp.arange(TAPS, dtype=jnp.int32)
    step_z = offset // 9 - 1
    step_y = offset // 3 % 3 - 1
    step_x = offset % 3 - 1
    layer = jnp.arange(LAYERS, dtype=jnp.int32)[:, None, None, None]
    column = jnp.arange(COLUMNS, dtype=jnp.int32)[None, :, None, None]
    within = jnp.arange(ZPS, dtype=jnp.int32)[None, None, :, None]
    target = within + step_z[None, None, None, :]
    layer_there = layer + jnp.floor_divide(target, ZPS)
    slot_there = jnp.mod(target, ZPS)
    column_there = column + step_x[None, None, None, :]
    inside = (layer_there >= 0) & (layer_there < LAYERS) & (column_there >= 0) & (column_there < COLUMNS)
    layer_safe = jnp.clip(layer_there, 0, LAYERS - 1)
    column_safe = jnp.clip(column_there, 0, COLUMNS - 1)
    there = present[layer_safe, column_safe, slot_there]
    row_there = rows[layer_safe, column_safe, slot_there]
    matches = row_there == rows[:, :, :, None] + step_y[None, None, None, :]
    valid = inside & there & matches & present[:, :, :, None]
    ident = (layer_safe * COLUMNS + column_safe) * ZPS + slot_there
    return jnp.where(valid, ident, -1).reshape(SLOTS, TAPS).astype(jnp.int32)


def draw_occupancy(key, part):
    present, rows = brick_layout(key)
    keys = jax.random.split(jax.random.fold_in(key, 5), 2)
    index = jnp.arange(SLOTS, dtype=jnp.int32)
    level = (jax.random.randint(keys[0], (SLOTS,), 0, 10) + 1) * 10
    level = jnp.where(index == 0, 100, level)
    level = jnp.where(present.reshape(SLOTS), level, 0)
    rolls = jax.random.randint(keys[1], (SLOTS, WORDS * 22), 0, 100)
    places = jnp.arange(WORDS * 22, dtype=jnp.int32)
    bit_table = jnp.logical_and(rolls < level[:, None], places[None, :] < VOX).astype(jnp.int32)
    weights_of_bits = jnp.left_shift(jnp.ones((22,), jnp.int32), jnp.arange(22, dtype=jnp.int32))
    packed = jnp.sum(bit_table.reshape(SLOTS, WORDS, 22) * weights_of_bits, axis=-1)
    return packed.astype(jnp.int32)


def shard_levels(key, dims, cuts, low, top_value):
    factor_of, own = 1.0, jax.random.fold_in(key, 6)
    for axis_at, parts in cuts:
        heights = jnp.exp(jax.random.uniform(jax.random.fold_in(own, axis_at), (parts,), jnp.float32, low / len(cuts), top_value / len(cuts)))
        factor_of = factor_of * jnp.repeat(heights, dims[axis_at] // parts).reshape([-1 if axis == axis_at else 1 for axis in range(len(dims))])
    return factor_of


def centred(stream_key, extent, width, most, cuts=(), kind=jnp.bfloat16):
    array = width * jax.random.normal(stream_key, extent, jnp.float32)
    if cuts:
        array = array * shard_levels(stream_key, extent, cuts, -0.22, 0.18)
    return jnp.clip(array, -most, most).astype(kind)


def setup_inputs(seed: int = 0) -> dict:
    key_of = jax.random.split(jax.random.key(seed), 6)
    features = centred(key_of[0], (SLOTS, C, VOX), 1.0, 6.0, ((0, 32),))
    weight = centred(key_of[1], (TAPS, C, C), (TAPS * C) ** -0.5, 0.15625)
    cotangent = centred(key_of[2], (SLOTS, C, VOX), 1.0, 6.0, ((0, 32),))
    occupancy = draw_occupancy(jax.random.fold_in(key_of[5], 71), 0)
    neighbours = draw_neighbours(jax.random.fold_in(key_of[5], 71), 0)
    return dict(features=features, weight=weight, cotangent=cotangent, occupancy=occupancy, neighbours=neighbours)


def unpack_bits(packed, voxels):
    places = jnp.arange(22, dtype=jnp.int32)
    bit_table = jnp.bitwise_and(jnp.right_shift(packed[..., :, None], places), 1)
    return bit_table.reshape(packed.shape[:-1] + (packed.shape[-1] * 22,))[..., :voxels]

def cut(length, side):
    if side < 0:
        return slice(length - 1, length)
    if side > 0:
        return slice(0, 1)
    return slice(0, length)

def assemble(blocks):
    layers = []
    for shift_z in (-1, 0, 1):
        rows = []
        for shift_y in (-1, 0, 1):
            columns = []
            for shift_x in (-1, 0, 1):
                offset = 9 * (shift_z + 1) + 3 * (shift_y + 1) + (shift_x + 1)
                columns.append(blocks[offset][:, cut(EDGE, shift_z), cut(EDGE, shift_y), cut(EDGE, shift_x)])
            rows.append(jnp.concatenate(columns, 3))
        layers.append(jnp.concatenate(rows, 2))
    return jnp.concatenate(layers, 1)

def windows(padded, direction):
    channels = padded.shape[0]
    pieces = []
    for shift_z in (-1, 0, 1):
        for shift_y in (-1, 0, 1):
            for shift_x in (-1, 0, 1):
                begin_z = 1 + direction * shift_z
                begin_y = 1 + direction * shift_y
                begin_x = 1 + direction * shift_x
                window = padded[:, begin_z:begin_z + EDGE, begin_y:begin_y + EDGE, begin_x:begin_x + EDGE]
                pieces.append(window.reshape(channels, EDGE * EDGE * EDGE))
    return jnp.stack(pieces, 0).reshape(27 * channels, EDGE * EDGE * EDGE)

def reference(features, weight, cotangent, occupancy, neighbours):
    occupied = unpack_bits(occupancy, VOX).astype(jnp.bfloat16)
    masked_input = features * occupied[:, None, :]
    masked_grad = cotangent * occupied[:, None, :]
    forward_matrix = jnp.transpose(weight, (1, 0, 2)).reshape(C, TAPS * C)
    backward_matrix = jnp.transpose(weight, (2, 0, 1)).reshape(C, TAPS * C)

    def one_slot(total, index):
        listed = neighbours[index]
        present = (listed >= 0).astype(jnp.bfloat16)[:, None, None]
        safe = jnp.maximum(listed, 0).astype(jnp.int32)
        near_input = (masked_input[safe] * present).reshape(TAPS, C, EDGE, EDGE, EDGE)
        near_grad = (masked_grad[safe] * present).reshape(TAPS, C, EDGE, EDGE, EDGE)
        input_patches = windows(assemble(near_input), 1)
        grad_patches = windows(assemble(near_grad), -1)
        scaling = occupied[index].astype(jnp.float32)[None, :]
        output_rows = jnp.dot(forward_matrix, input_patches, preferred_element_type=jnp.float32)
        output_rows = (output_rows * scaling).astype(jnp.bfloat16)
        grad_rows = jnp.dot(backward_matrix, grad_patches, preferred_element_type=jnp.float32)
        grad_rows = (grad_rows * scaling).astype(jnp.bfloat16)
        term = lax.dot_general(masked_grad[index], input_patches, (((1,), (1,)), ((), ())), preferred_element_type=jnp.float32)
        return (total + term, (output_rows, grad_rows))
    start = jnp.zeros((C, TAPS * C), jnp.float32)
    total, (output, grad_input) = lax.scan(one_slot, start, jnp.arange(SLOTS, dtype=jnp.int32))
    grad_weight = jnp.transpose(total.reshape(C, TAPS, C), (1, 0, 2)) / math.sqrt(VOX * SLOTS)
    return (output, grad_input, grad_weight.astype(jnp.float32))
```

```python
import functools
import math

import jax
import jax.numpy as jnp
import numpy as np
from jax import lax
from jax.experimental import pallas as pl
from jax.experimental.pallas import tpu as pltpu
from jax.sharding import PartitionSpec as P

EDGE = 8
PITCH = EDGE + 2
FACE = EDGE * EDGE
LANES = 128
BITS = 22
GROUP = 8
MESH = pl.DeviceIdType.MESH
F32 = jnp.float32
BF16 = jnp.bfloat16


def point(y, x):
    return PITCH * (y + 1) + (x + 1)


def tables(words, voxels):
    pick = np.zeros((voxels, 2 * FACE), np.float32)
    for z in range(EDGE):
        for y in range(EDGE):
            pick[z * FACE + y * EDGE, z * EDGE + y] = 1
            pick[z * FACE + y * EDGE + EDGE - 1, FACE + z * EDGE + y] = 1
    spread = np.zeros((EDGE // 2, 2 * LANES, 2 * LANES), np.float32)
    pack = np.zeros((2 * LANES, LANES), np.float32)
    for half in range(2):
        base = half * LANES
        for y in range(EDGE):
            rows = [y] + ([-1] if y == EDGE - 1 else []) + ([EDGE] if y == 0 else [])
            for x in range(EDGE):
                lane = half * FACE + y * EDGE + x
                pack[base + point(y, x), lane] = 1
                for row in rows:
                    spread[:, lane, base + point(row, x)] = 1
            for pair in range(EDGE // 2):
                z = 2 * pair + half
                for row in rows:
                    spread[pair, LANES + z * EDGE + y, base + point(row, -1)] = 1
                    spread[pair, LANES + FACE + z * EDGE + y, base + point(row, EDGE)] = 1
    to_voxel = np.zeros((words, voxels), np.float32)
    to_voxel[np.arange(voxels) // BITS, np.arange(voxels)] = 1
    region = np.zeros((27, 3 * LANES), np.float32)
    inside = np.zeros((1, LANES), np.float32)
    for y in range(-1, EDGE + 1):
        for x in range(-1, EDGE + 1):
            c = 0 if y < 0 else (2 if y == EDGE else 1)
            e = 0 if x < 0 else (2 if x == EDGE else 1)
            for a in range(3):
                region[9 * a + 3 * c + e, a * LANES + point(y, x)] = 1
            if c == 1 and e == 1:
                inside[0, point(y, x)] = 1
    return pick, spread, pack, to_voxel, region, inside


def kernel(
    n_slab, n_brick, scale,
    features, weight, cotangent, occupancy, neighbours,
    pick, spread, pack, to_voxel, region, inside, unit,
    output, grad_input, grad_weight,
    cube, faces, arrived, planes, patches_in, patches_grad, shifted, forward, backward,
    part, landed, reduced, across, final, total,
    x_send, x_recv, z_send, z_recv, rs_send, rs_recv, b_send, b_recv, ag_send, ag_recv,
):
    slots, channels, voxels = features.shape
    s = lax.axis_index("slab")
    t = lax.axis_index("brick")
    per_row = GROUP // n_slab
    blocks = n_brick // per_row
    column = lax.rem(t, per_row)
    block = t // per_row
    member = s * per_row + column

    def group_device(i):
        other = lax.rem(member + i, GROUP)
        return other, (other // per_row, block * per_row + lax.rem(other, per_row))

    def block_device(i):
        return (s, lax.rem(block + i, blocks) * per_row + column)

    has_left, has_right = t > 0, t < n_brick - 1
    has_below, has_above = s > 0, s < n_slab - 1
    sides = (
        (has_left, (s, t - 1)),
        (has_right, (s, t + 1)),
        (has_below, (s - 1, t)),
        (has_above, (s + 1, t)),
    )
    barrier = pltpu.get_barrier_semaphore()
    for there, device in sides:
        @pl.when(there)
        def _():
            pl.semaphore_signal(barrier, inc=1, device_id=device, device_id_type=MESH)
    for i in range(1, GROUP):
        pl.semaphore_signal(barrier, inc=1, device_id=group_device(i)[1], device_id_type=MESH)
    for i in range(1, blocks):
        pl.semaphore_signal(barrier, inc=1, device_id=block_device(i), device_id_type=MESH)

    packed = occupancy[...]
    words = jnp.zeros((slots, voxels), jnp.int32)
    for shift in (0, 8, 16):
        byte = jnp.bitwise_and(jnp.right_shift(packed, shift), 255).astype(F32)
        spread_byte = jnp.dot(byte, to_voxel[...], preferred_element_type=F32)
        words = words + jnp.left_shift(spread_byte.astype(jnp.int32), shift)
    place = lax.rem(lax.broadcasted_iota(jnp.int32, (slots, voxels), 1), BITS)
    occupied = jnp.bitwise_and(jnp.right_shift(words, place), 1).astype(F32).astype(BF16)
    ends = []
    for j in range(slots):
        cube[j, :channels, :] = features[j] * occupied[j : j + 1, :]
        cube[j, channels:, :] = cotangent[j] * occupied[j : j + 1, :]
        ends.append(jnp.dot(cube[j], pick[...], preferred_element_type=F32).astype(BF16))
    faces[0] = jnp.concatenate([end[:, :FACE] for end in ends], 1)
    faces[1] = jnp.concatenate([end[:, FACE:] for end in ends], 1)

    beside = (t + n_brick - 1) // n_brick + (2 * n_brick - 2 - t) // n_brick
    upright = (s + n_slab - 1) // n_slab + (2 * n_slab - 2 - s) // n_slab
    pl.semaphore_wait(barrier, GROUP - 1 + blocks - 1 + beside + upright)

    to_left = pltpu.make_async_remote_copy(
        src_ref=faces.at[0], dst_ref=arrived.at[1], send_sem=x_send.at[0], recv_sem=x_recv.at[1],
        device_id=(s, t - 1), device_id_type=MESH)
    to_right = pltpu.make_async_remote_copy(
        src_ref=faces.at[1], dst_ref=arrived.at[0], send_sem=x_send.at[1], recv_sem=x_recv.at[0],
        device_id=(s, t + 1), device_id_type=MESH)

    @pl.when(has_left)
    def _():
        to_left.start()

    @pl.when(has_right)
    def _():
        to_right.start()

    for k in range(27):
        a, ce = k // 9, k % 9
        forward[a * channels : (a + 1) * channels, ce * channels : (ce + 1) * channels] = weight[k]
    turned = lax.dot_general(
        unit[...], weight[...].reshape(27 * channels, channels), (((1,), (1,)), ((), ())),
        preferred_element_type=F32).astype(BF16)
    for a in range(3):
        backward[a * channels : (a + 1) * channels, :] = turned[:, a * 9 * channels : (a + 1) * 9 * channels]
    present = jnp.where(neighbours[...] >= 0, 1.0, 0.0).astype(F32)
    masks = jnp.dot(present, region[...], preferred_element_type=F32).astype(BF16)
    shifted[...] = jnp.zeros(shifted.shape, BF16)

    @pl.when(jnp.logical_not(has_left))
    def _():
        arrived[0] = jnp.zeros(arrived.shape[1:], BF16)

    @pl.when(jnp.logical_not(has_right))
    def _():
        arrived[1] = jnp.zeros(arrived.shape[1:], BF16)

    @pl.when(jnp.logical_not(has_below))
    def _():
        planes[0] = jnp.zeros(planes.shape[1:], BF16)

    @pl.when(jnp.logical_not(has_above))
    def _():
        planes[slots * EDGE + 1] = jnp.zeros(planes.shape[1:], BF16)

    @pl.when(has_right)
    def _():
        to_left.wait_recv()

    @pl.when(has_left)
    def _():
        to_right.wait_recv()

    def spread_pair(j, pair):
        beside = jnp.concatenate(
            [arrived[0][:, j * FACE : (j + 1) * FACE], arrived[1][:, j * FACE : (j + 1) * FACE]], 1)
        both = jnp.concatenate([cube[j, :, pair * LANES : (pair + 1) * LANES], beside], 1)
        wide = jnp.dot(both, spread[pair], preferred_element_type=F32).astype(BF16)
        planes[1 + j * EDGE + 2 * pair] = wide[:, :LANES]
        planes[2 + j * EDGE + 2 * pair] = wide[:, LANES:]

    to_above = pltpu.make_async_remote_copy(
        src_ref=planes.at[slots * EDGE], dst_ref=planes.at[0], send_sem=z_send.at[0], recv_sem=z_recv.at[0],
        device_id=(s + 1, t), device_id_type=MESH)
    to_below = pltpu.make_async_remote_copy(
        src_ref=planes.at[1], dst_ref=planes.at[slots * EDGE + 1], send_sem=z_send.at[1], recv_sem=z_recv.at[1],
        device_id=(s - 1, t), device_id_type=MESH)
    spread_pair(slots - 1, EDGE // 2 - 1)

    @pl.when(has_above)
    def _():
        to_above.start()

    spread_pair(0, 0)

    @pl.when(has_below)
    def _():
        to_below.start()

    for j in range(slots):
        for pair in range(EDGE // 2):
            if (j, pair) not in ((0, 0), (slots - 1, EDGE // 2 - 1)):
                spread_pair(j, pair)

    def make_patches(j, layer):
        kind = 0 if layer == 0 else (2 if layer == EDGE + 1 else 1)
        plane = planes[j * EDGE + layer] * masks[j : j + 1, kind * LANES : (kind + 1) * LANES]
        lanes = slice(layer * LANES, (layer + 1) * LANES)
        top, bottom = plane[:channels].astype(F32), plane[channels:].astype(F32)
        for ce in range(9):
            step = PITCH * (ce // 3 - 1) + (ce % 3 - 1)
            rows = slice(ce * channels, (ce + 1) * channels)
            moved = top if step == 0 else pltpu.roll(top, (-step) % LANES, 1)
            patches_in[j, rows, lanes] = moved.astype(BF16)
            moved = bottom if step == 0 else pltpu.roll(bottom, step % LANES, 1)
            patches_grad[j, rows, lanes] = moved.astype(BF16)
        if kind == 1:
            own = plane[channels:] * inside[...]
            for a in range(3):
                at = layer + a - 1
                shifted[j, a * channels : (a + 1) * channels, at * LANES : (at + 1) * LANES] = own

    for j in range(slots):
        for layer in range(EDGE + 2):
            if (j, layer) not in ((0, 0), (slots - 1, EDGE + 1)):
                make_patches(j, layer)

    @pl.when(has_below)
    def _():
        to_above.wait_recv()

    @pl.when(has_above)
    def _():
        to_below.wait_recv()

    make_patches(0, 0)
    make_patches(slots - 1, EDGE + 1)

    terms = None
    for j in range(slots):
        term = lax.dot_general(
            shifted[j], patches_in[j], (((1,), (1,)), ((), ())), preferred_element_type=F32)
        terms = term if terms is None else terms + term
    part[...] = terms.reshape(part.shape)

    scatters = []
    for i in range(1, GROUP):
        other, device = group_device(i)
        copy = pltpu.make_async_remote_copy(
            src_ref=part.at[other], dst_ref=landed.at[i - 1],
            send_sem=rs_send.at[i - 1], recv_sem=rs_recv.at[i - 1], device_id=device, device_id_type=MESH)
        copy.start()
        scatters.append(copy)

    span = EDGE * LANES

    def convolve(j):
        wide = jnp.dot(forward[...], patches_in[j], preferred_element_type=F32)
        rows = [wide[a * channels : (a + 1) * channels, a * LANES : a * LANES + span] for a in range(3)]
        ahead = (rows[0] + rows[1] + rows[2]).astype(BF16)
        wide = jnp.dot(backward[...], patches_grad[j], preferred_element_type=F32)
        rows = [wide[a * channels : (a + 1) * channels, (2 - a) * LANES : (2 - a) * LANES + span] for a in range(3)]
        back = (rows[0] + rows[1] + rows[2]).astype(BF16)
        both = jnp.concatenate([ahead, back], 0)
        for pair in range(EDGE // 2):
            lanes = slice(pair * LANES, (pair + 1) * LANES)
            close = jnp.dot(
                both[:, 2 * pair * LANES : 2 * (pair + 1) * LANES], pack[...], preferred_element_type=F32)
            close = close.astype(BF16) * occupied[j : j + 1, lanes]
            output[j, :, lanes] = close[:channels]
            grad_input[j, :, lanes] = close[channels:]

    convolve(0)
    mine = part[member]
    for copy in scatters:
        copy.wait_recv()
    for i in range(GROUP - 1):
        mine = mine + landed[i]
    reduced[...] = mine
    exchanges = []
    for i in range(1, blocks):
        copy = pltpu.make_async_remote_copy(
            src_ref=reduced, dst_ref=across.at[i - 1],
            send_sem=b_send.at[i - 1], recv_sem=b_recv.at[i - 1], device_id=block_device(i), device_id_type=MESH)
        copy.start()
        exchanges.append(copy)
    for j in range(1, slots):
        convolve(j)
    whole = reduced[...]
    for copy in exchanges:
        copy.wait_recv()
    for i in range(blocks - 1):
        whole = whole + across[i]
    whole = whole * scale
    final[...] = whole
    gathers = []
    for i in range(1, GROUP):
        copy = pltpu.make_async_remote_copy(
            src_ref=final, dst_ref=total.at[member],
            send_sem=ag_send.at[i - 1], recv_sem=ag_recv.at[i - 1], device_id=group_device(i)[1], device_id_type=MESH)
        copy.start()
        gathers.append(copy)
    total[member] = whole

    @pl.when(has_left)
    def _():
        to_left.wait_send()

    @pl.when(has_right)
    def _():
        to_right.wait_send()

    @pl.when(has_above)
    def _():
        to_above.wait_send()

    @pl.when(has_below)
    def _():
        to_below.wait_send()

    for copy in scatters + exchanges:
        copy.wait_send()
    for copy in gathers:
        copy.wait()
    everything = total[...].reshape(3 * channels, 9 * channels)
    for k in range(27):
        a, ce = k // 9, k % 9
        grad_weight[k] = everything[a * channels : (a + 1) * channels, ce * channels : (ce + 1) * channels]


def solution(mesh):
    n_slab, n_brick = mesh.shape["slab"], mesh.shape["brick"]

    def per_device(features, weight, cotangent, occupancy, neighbours):
        slots, channels, voxels = features.shape
        pick, spread, pack, to_voxel, region, inside = tables(occupancy.shape[1], voxels)
        constants = (
            jnp.asarray(pick, BF16), jnp.asarray(spread, BF16), jnp.asarray(pack, BF16),
            jnp.asarray(to_voxel, F32), jnp.asarray(region, F32), jnp.asarray(inside, BF16),
            jnp.asarray(np.eye(channels), BF16),
        )
        scale = 1.0 / math.sqrt(voxels * slots * n_slab * n_brick)
        blocks = n_brick * n_slab // GROUP
        wide = 2 * channels
        share = (3 * channels // GROUP, 9 * channels)
        padded = (EDGE + 2) * LANES
        dma = pltpu.SemaphoreType.DMA
        return pl.pallas_call(
            functools.partial(kernel, n_slab, n_brick, scale),
            out_shape=(
                jax.ShapeDtypeStruct(features.shape, BF16),
                jax.ShapeDtypeStruct(features.shape, BF16),
                jax.ShapeDtypeStruct(weight.shape, F32),
            ),
            in_specs=[pl.BlockSpec(memory_space=pltpu.VMEM)] * 12,
            out_specs=[pl.BlockSpec(memory_space=pltpu.VMEM)] * 3,
            scratch_shapes=[
                pltpu.VMEM((slots, wide, voxels), BF16),
                pltpu.VMEM((2, wide, slots * FACE), BF16),
                pltpu.VMEM((2, wide, slots * FACE), BF16),
                pltpu.VMEM((slots * EDGE + 2, wide, LANES), BF16),
                pltpu.VMEM((slots, 9 * channels, padded), BF16),
                pltpu.VMEM((slots, 9 * channels, padded), BF16),
                pltpu.VMEM((slots, 3 * channels, padded), BF16),
                pltpu.VMEM((3 * channels, 9 * channels), BF16),
                pltpu.VMEM((3 * channels, 9 * channels), BF16),
                pltpu.VMEM((GROUP,) + share, F32),
                pltpu.VMEM((GROUP - 1,) + share, F32),
                pltpu.VMEM(share, F32),
                pltpu.VMEM((blocks - 1,) + share, F32),
                pltpu.VMEM(share, F32),
                pltpu.VMEM((GROUP,) + share, F32),
                dma((2,)), dma((2,)), dma((2,)), dma((2,)),
                dma((GROUP - 1,)), dma((GROUP - 1,)),
                dma((blocks - 1,)), dma((blocks - 1,)),
                dma((GROUP - 1,)), dma((GROUP - 1,)),
            ],
            compiler_params=pltpu.CompilerParams(
                collective_id=0, has_side_effects=True, vmem_limit_bytes=40 * 1024 * 1024
            ),
        )(features, weight, cotangent, occupancy, neighbours, *constants)

    placed = (
        P(("slab", "brick"), None, None),
        P(),
        P(("slab", "brick"), None, None),
        P(("slab", "brick"), None),
        P(("slab", "brick"), None),
    )
    return jax.shard_map(
        per_device,
        mesh=mesh,
        in_specs=placed,
        out_specs=(P(("slab", "brick"), None, None), P(("slab", "brick"), None, None), P()),
        check_vma=False,
    )
```

```python
import functools
import math

import jax
import jax.numpy as jnp
import numpy as np
from jax import lax
from jax.experimental import pallas as pl
from jax.experimental.pallas import tpu as pltpu
from jax.sharding import PartitionSpec as P

EDGE = 8
PITCH = EDGE + 2
FACE = EDGE * EDGE
LANES = 128
BITS = 22
GROUP = 8
ORDER = (1, 0, 2)
MESH = pl.DeviceIdType.MESH
F32 = jnp.float32
BF16 = jnp.bfloat16


def point(y, x):
    return PITCH * (y + 1) + (x + 1)


def tables(words, voxels):
    pick = np.zeros((voxels, 2 * FACE), np.float32)
    for z in range(EDGE):
        for y in range(EDGE):
            pick[z * FACE + y * EDGE, z * EDGE + y] = 1
            pick[z * FACE + y * EDGE + EDGE - 1, FACE + z * EDGE + y] = 1
    spread = np.zeros((EDGE // 2, 2 * LANES, 2 * LANES), np.float32)
    pack = np.zeros((2 * LANES, LANES), np.float32)
    for half in range(2):
        base = half * LANES
        for y in range(EDGE):
            rows = [y] + ([-1] if y == EDGE - 1 else []) + ([EDGE] if y == 0 else [])
            for x in range(EDGE):
                lane = half * FACE + y * EDGE + x
                pack[base + point(y, x), lane] = 1
                for row in rows:
                    spread[:, lane, base + point(row, x)] = 1
            for pair in range(EDGE // 2):
                z = 2 * pair + half
                for row in rows:
                    spread[pair, LANES + z * EDGE + y, base + point(row, -1)] = 1
                    spread[pair, LANES + FACE + z * EDGE + y, base + point(row, EDGE)] = 1
    to_voxel = np.zeros((words, voxels), np.float32)
    to_voxel[np.arange(voxels) // BITS, np.arange(voxels)] = 1
    region = np.zeros((27, 3 * LANES), np.float32)
    inside = np.zeros((1, LANES), np.float32)
    for y in range(-1, EDGE + 1):
        for x in range(-1, EDGE + 1):
            c = 0 if y < 0 else (2 if y == EDGE else 1)
            e = 0 if x < 0 else (2 if x == EDGE else 1)
            for a in range(3):
                region[9 * a + 3 * c + e, a * LANES + point(y, x)] = 1
            if c == 1 and e == 1:
                inside[0, point(y, x)] = 1
    return pick, spread, pack, to_voxel, region, inside


def kernel(
    n_slab, n_brick, scale, count, *refs,
):
    sources, refs = refs[:count], refs[count:]
    (output, grad_input, grad_weight), held, refs = refs[:3], refs[3 : 3 + count], refs[3 + count :]
    (
        features, cotangent, occupancy, pick, to_voxel, weight, unit, neighbours, region, spread, inside, pack,
    ) = held
    (
    cube, faces, arrived, planes, patches_in, patches_grad, interior, forward, backward,
    part, landed, reduced, across, final, total,
    x_send, x_recv, z_send, z_recv, rs_send, rs_recv, b_send, b_recv, ag_send, ag_recv, in_sems,
    ) = refs
    loads = [pltpu.make_async_copy(sources[i], held[i], in_sems.at[i]) for i in range(count)]
    for load in loads:
        load.start()
    slots, channels, voxels = features.shape
    s = lax.axis_index("slab")
    t = lax.axis_index("brick")
    per_row = GROUP // n_slab
    blocks = n_brick // per_row
    column = lax.rem(t, per_row)
    block = t // per_row
    member = s * per_row + column

    def group_device(i):
        other = lax.rem(member + i, GROUP)
        return other, (other // per_row, block * per_row + lax.rem(other, per_row))

    def block_device(i):
        return (s, lax.rem(block + i, blocks) * per_row + column)

    has_left, has_right = t > 0, t < n_brick - 1
    has_below, has_above = s > 0, s < n_slab - 1
    sides = (
        (has_left, (s, t - 1)),
        (has_right, (s, t + 1)),
        (has_below, (s - 1, t)),
        (has_above, (s + 1, t)),
    )
    barrier = pltpu.get_barrier_semaphore()
    for there, device in sides:
        @pl.when(there)
        def _():
            pl.semaphore_signal(barrier, inc=1, device_id=device, device_id_type=MESH)
    for i in range(1, GROUP):
        pl.semaphore_signal(barrier, inc=1, device_id=group_device(i)[1], device_id_type=MESH)
    for i in range(1, blocks):
        pl.semaphore_signal(barrier, inc=1, device_id=block_device(i), device_id_type=MESH)

    for load in loads[:5]:
        load.wait()
    packed = occupancy[...]
    words = jnp.zeros((slots, voxels), jnp.int32)
    for shift in (0, 8, 16):
        byte = jnp.bitwise_and(jnp.right_shift(packed, shift), 255).astype(F32)
        spread_byte = jnp.dot(byte, to_voxel[...], preferred_element_type=F32)
        words = words + jnp.left_shift(spread_byte.astype(jnp.int32), shift)
    place = lax.rem(lax.broadcasted_iota(jnp.int32, (slots, voxels), 1), BITS)
    occupied = jnp.bitwise_and(jnp.right_shift(words, place), 1).astype(F32).astype(BF16)
    ends = []
    for j in range(slots):
        cube[j, :channels, :] = features[j] * occupied[j : j + 1, :]
        cube[j, channels:, :] = cotangent[j] * occupied[j : j + 1, :]
        ends.append(jnp.dot(cube[j], pick[...], preferred_element_type=F32).astype(BF16))
    faces[0] = jnp.concatenate([end[:, :FACE] for end in ends], 1)
    faces[1] = jnp.concatenate([end[:, FACE:] for end in ends], 1)

    beside = (t + n_brick - 1) // n_brick + (2 * n_brick - 2 - t) // n_brick
    upright = (s + n_slab - 1) // n_slab + (2 * n_slab - 2 - s) // n_slab
    pl.semaphore_wait(barrier, GROUP - 1 + blocks - 1 + beside + upright)

    to_left = pltpu.make_async_remote_copy(
        src_ref=faces.at[0], dst_ref=arrived.at[1], send_sem=x_send.at[0], recv_sem=x_recv.at[1],
        device_id=(s, t - 1), device_id_type=MESH)
    to_right = pltpu.make_async_remote_copy(
        src_ref=faces.at[1], dst_ref=arrived.at[0], send_sem=x_send.at[1], recv_sem=x_recv.at[0],
        device_id=(s, t + 1), device_id_type=MESH)

    @pl.when(has_left)
    def _():
        to_left.start()

    @pl.when(has_right)
    def _():
        to_right.start()

    for load in loads[5:]:
        load.wait()
    for k in range(27):
        a, ce = k // 9, k % 9
        forward[a * channels : (a + 1) * channels, ce * channels : (ce + 1) * channels] = weight[k]
    turned = lax.dot_general(
        unit[...], weight[...].reshape(27 * channels, channels), (((1,), (1,)), ((), ())),
        preferred_element_type=F32).astype(BF16)
    for a in range(3):
        backward[a * channels : (a + 1) * channels, :] = turned[:, a * 9 * channels : (a + 1) * 9 * channels]
    present = jnp.where(neighbours[...] >= 0, 1.0, 0.0).astype(F32)
    masks = jnp.dot(present, region[...], preferred_element_type=F32).astype(BF16)

    @pl.when(jnp.logical_not(has_left))
    def _():
        arrived[0] = jnp.zeros(arrived.shape[1:], BF16)

    @pl.when(jnp.logical_not(has_right))
    def _():
        arrived[1] = jnp.zeros(arrived.shape[1:], BF16)

    @pl.when(jnp.logical_not(has_below))
    def _():
        planes[0] = jnp.zeros(planes.shape[1:], BF16)

    @pl.when(jnp.logical_not(has_above))
    def _():
        planes[slots * EDGE + 1] = jnp.zeros(planes.shape[1:], BF16)

    @pl.when(has_right)
    def _():
        to_left.wait_recv()

    @pl.when(has_left)
    def _():
        to_right.wait_recv()

    def spread_pair(j, pair):
        beside = jnp.concatenate(
            [arrived[0][:, j * FACE : (j + 1) * FACE], arrived[1][:, j * FACE : (j + 1) * FACE]], 1)
        both = jnp.concatenate([cube[j, :, pair * LANES : (pair + 1) * LANES], beside], 1)
        wide = jnp.dot(both, spread[pair], preferred_element_type=F32).astype(BF16)
        planes[1 + j * EDGE + 2 * pair] = wide[:, :LANES]
        planes[2 + j * EDGE + 2 * pair] = wide[:, LANES:]

    to_above = pltpu.make_async_remote_copy(
        src_ref=planes.at[slots * EDGE], dst_ref=planes.at[0], send_sem=z_send.at[0], recv_sem=z_recv.at[0],
        device_id=(s + 1, t), device_id_type=MESH)
    to_below = pltpu.make_async_remote_copy(
        src_ref=planes.at[1], dst_ref=planes.at[slots * EDGE + 1], send_sem=z_send.at[1], recv_sem=z_recv.at[1],
        device_id=(s - 1, t), device_id_type=MESH)
    spread_pair(slots - 1, EDGE // 2 - 1)

    @pl.when(has_above)
    def _():
        to_above.start()

    spread_pair(0, 0)

    @pl.when(has_below)
    def _():
        to_below.start()

    for j in range(slots):
        for pair in range(EDGE // 2):
            if (j, pair) not in ((0, 0), (slots - 1, EDGE // 2 - 1)):
                spread_pair(j, pair)

    def make_patches(j, layer):
        kind = 0 if layer == 0 else (2 if layer == EDGE + 1 else 1)
        plane = planes[j * EDGE + layer] * masks[j : j + 1, kind * LANES : (kind + 1) * LANES]
        lanes = slice(layer * LANES, (layer + 1) * LANES)
        top, bottom = plane[:channels].astype(F32), plane[channels:].astype(F32)
        for ce in range(9):
            step = PITCH * (ce // 3 - 1) + (ce % 3 - 1)
            rows = slice(ce * channels, (ce + 1) * channels)
            moved = top if step == 0 else pltpu.roll(top, (-step) % LANES, 1)
            patches_in[j, rows, lanes] = moved.astype(BF16)
            moved = bottom if step == 0 else pltpu.roll(bottom, step % LANES, 1)
            patches_grad[j, rows, lanes] = moved.astype(BF16)
        if kind == 1:
            interior[j, :, (layer - 1) * LANES : layer * LANES] = plane[channels:] * inside[...]

    for j in range(slots):
        for layer in range(EDGE + 2):
            if (j, layer) not in ((0, 0), (slots - 1, EDGE + 1)):
                make_patches(j, layer)

    span = EDGE * LANES
    scatters = [[], [], []]

    def scatter(a):
        terms = None
        for j in range(slots):
            term = lax.dot_general(
                interior[j], patches_in[j, :, a * LANES : a * LANES + span], (((1,), (1,)), ((), ())),
                preferred_element_type=F32)
            terms = term if terms is None else terms + term
        part[a] = terms.reshape(part.shape[1:])
        for i in range(1, GROUP):
            other, device = group_device(i)
            copy = pltpu.make_async_remote_copy(
                src_ref=part.at[a, other], dst_ref=landed.at[a, i - 1],
                send_sem=rs_send.at[a, i - 1], recv_sem=rs_recv.at[a, i - 1], device_id=device, device_id_type=MESH)
            copy.start()
            scatters[a].append(copy)

    scatter(1)

    @pl.when(has_below)
    def _():
        to_above.wait_recv()

    make_patches(0, 0)
    scatter(0)

    @pl.when(has_above)
    def _():
        to_below.wait_recv()

    make_patches(slots - 1, EDGE + 1)
    scatter(2)

    def convolve(j):
        wide = jnp.dot(forward[...], patches_in[j], preferred_element_type=F32)
        rows = [wide[a * channels : (a + 1) * channels, a * LANES : a * LANES + span] for a in range(3)]
        ahead = (rows[0] + rows[1] + rows[2]).astype(BF16)
        wide = jnp.dot(backward[...], patches_grad[j], preferred_element_type=F32)
        rows = [wide[a * channels : (a + 1) * channels, (2 - a) * LANES : (2 - a) * LANES + span] for a in range(3)]
        back = (rows[0] + rows[1] + rows[2]).astype(BF16)
        both = jnp.concatenate([ahead, back], 0)
        for pair in range(EDGE // 2):
            lanes = slice(pair * LANES, (pair + 1) * LANES)
            close = jnp.dot(
                both[:, 2 * pair * LANES : 2 * (pair + 1) * LANES], pack[...], preferred_element_type=F32)
            close = close.astype(BF16) * occupied[j : j + 1, lanes]
            output[j, :, lanes] = close[:channels]
            grad_input[j, :, lanes] = close[channels:]

    convolve(0)
    exchanges = [[], [], []]
    for a in ORDER:
        mine = part[a, member]
        for copy in scatters[a]:
            copy.wait_recv()
        for i in range(GROUP - 1):
            mine = mine + landed[a, i]
        reduced[a] = mine
        for i in range(1, blocks):
            copy = pltpu.make_async_remote_copy(
                src_ref=reduced.at[a], dst_ref=across.at[a, i - 1],
                send_sem=b_send.at[a, i - 1], recv_sem=b_recv.at[a, i - 1],
                device_id=block_device(i), device_id_type=MESH)
            copy.start()
            exchanges[a].append(copy)
    for j in range(1, slots):
        convolve(j)
    gathers = [[], [], []]
    for a in ORDER:
        whole = reduced[a]
        for copy in exchanges[a]:
            copy.wait_recv()
        for i in range(blocks - 1):
            whole = whole + across[a, i]
        whole = whole * scale
        final[a] = whole
        for i in range(1, GROUP):
            copy = pltpu.make_async_remote_copy(
                src_ref=final.at[a], dst_ref=total.at[a, member],
                send_sem=ag_send.at[a, i - 1], recv_sem=ag_recv.at[a, i - 1],
                device_id=group_device(i)[1], device_id_type=MESH)
            copy.start()
            gathers[a].append(copy)
        total[a, member] = whole

    @pl.when(has_left)
    def _():
        to_left.wait_send()

    @pl.when(has_right)
    def _():
        to_right.wait_send()

    @pl.when(has_above)
    def _():
        to_above.wait_send()

    @pl.when(has_below)
    def _():
        to_below.wait_send()

    for a in ORDER:
        for copy in scatters[a] + exchanges[a]:
            copy.wait_send()
    for a in ORDER:
        for copy in gathers[a]:
            copy.wait()
        rows = total[a].reshape(channels, 9 * channels)
        for ce in range(9):
            grad_weight[9 * a + ce] = rows[:, ce * channels : (ce + 1) * channels]


def place(*refs):
    count = 3
    sources, results, held = refs[:count], refs[count : 2 * count], refs[2 * count : 3 * count]
    load_sems, store_sems = refs[3 * count :]
    loads = [pltpu.make_async_copy(sources[i], held[i], load_sems.at[i]) for i in range(count)]
    stores = [pltpu.make_async_copy(held[i], results[i], store_sems.at[i]) for i in range(count)]
    for load in loads:
        load.start()
    for load, store in zip(loads, stores):
        load.wait()
        store.start()
    for store in stores:
        store.wait()


def solution(mesh):
    n_slab, n_brick = mesh.shape["slab"], mesh.shape["brick"]

    def per_device(features, weight, cotangent, occupancy, neighbours):
        slots, channels, voxels = features.shape
        pick, spread, pack, to_voxel, region, inside = tables(occupancy.shape[1], voxels)
        sources = (
            features, cotangent, occupancy, jnp.asarray(pick, BF16), jnp.asarray(to_voxel, F32),
            weight, jnp.asarray(np.eye(channels), BF16), neighbours, jnp.asarray(region, F32),
            jnp.asarray(spread, BF16), jnp.asarray(inside, BF16), jnp.asarray(pack, BF16),
        )
        count = len(sources)
        scale = 1.0 / math.sqrt(voxels * slots * n_slab * n_brick)
        blocks = n_brick * n_slab // GROUP
        wide = 2 * channels
        share = (channels // GROUP, 9 * channels)
        padded = (EDGE + 2) * LANES
        dma = pltpu.SemaphoreType.DMA
        results = pl.pallas_call(
            functools.partial(kernel, n_slab, n_brick, scale, count),
            out_shape=(
                jax.ShapeDtypeStruct(features.shape, BF16),
                jax.ShapeDtypeStruct(features.shape, BF16),
                jax.ShapeDtypeStruct(weight.shape, F32),
            ),
            in_specs=[pl.BlockSpec(memory_space=pltpu.HBM)] * count,
            out_specs=[pl.BlockSpec(memory_space=pltpu.VMEM)] * 3,
            scratch_shapes=[pltpu.VMEM(source.shape, source.dtype) for source in sources] + [
                pltpu.VMEM((slots, wide, voxels), BF16),
                pltpu.VMEM((2, wide, slots * FACE), BF16),
                pltpu.VMEM((2, wide, slots * FACE), BF16),
                pltpu.VMEM((slots * EDGE + 2, wide, LANES), BF16),
                pltpu.VMEM((slots, 9 * channels, padded), BF16),
                pltpu.VMEM((slots, 9 * channels, padded), BF16),
                pltpu.VMEM((slots, channels, EDGE * LANES), BF16),
                pltpu.VMEM((3 * channels, 9 * channels), BF16),
                pltpu.VMEM((3 * channels, 9 * channels), BF16),
                pltpu.VMEM((3, GROUP) + share, F32),
                pltpu.VMEM((3, GROUP - 1) + share, F32),
                pltpu.VMEM((3,) + share, F32),
                pltpu.VMEM((3, blocks - 1) + share, F32),
                pltpu.VMEM((3,) + share, F32),
                pltpu.VMEM((3, GROUP) + share, F32),
                dma((2,)), dma((2,)), dma((2,)), dma((2,)),
                dma((3, GROUP - 1)), dma((3, GROUP - 1)),
                dma((3, blocks - 1)), dma((3, blocks - 1)),
                dma((3, GROUP - 1)), dma((3, GROUP - 1)), dma((count,)),
            ],
            compiler_params=pltpu.CompilerParams(
                collective_id=0, has_side_effects=True, vmem_limit_bytes=63 * 1024 * 1024
            ),
        )(*sources)
        return pl.pallas_call(
            place,
            out_shape=tuple(jax.ShapeDtypeStruct(result.shape, result.dtype) for result in results),
            in_specs=[pl.BlockSpec(memory_space=pltpu.HBM)] * 3,
            out_specs=[pl.BlockSpec(memory_space=pltpu.HBM)] * 3,
            scratch_shapes=[pltpu.VMEM(result.shape, result.dtype) for result in results] + [dma((3,)), dma((3,))],
            compiler_params=pltpu.CompilerParams(vmem_limit_bytes=63 * 1024 * 1024),
        )(*results)

    placed = (
        P(("slab", "brick"), None, None),
        P(),
        P(("slab", "brick"), None, None),
        P(("slab", "brick"), None),
        P(("slab", "brick"), None),
    )
    return jax.shard_map(
        per_device,
        mesh=mesh,
        in_specs=placed,
        out_specs=(P(("slab", "brick"), None, None), P(("slab", "brick"), None, None), P()),
        check_vma=False,
    )
```

```python
import functools
import math

import jax
import jax.numpy as jnp
import numpy as np
from jax import lax
from jax.experimental import pallas as pl
from jax.experimental.pallas import tpu as pltpu
from jax.sharding import PartitionSpec as P

EDGE = 8
PITCH = EDGE + 2
FACE = EDGE * EDGE
LANES = 128
BITS = 22
GROUP = 8
ORDER = (1, 0, 2)
MESH = pl.DeviceIdType.MESH
F32 = jnp.float32
BF16 = jnp.bfloat16


def point(y, x):
    return PITCH * (y + 1) + (x + 1)


def tables(words, voxels):
    pick = np.zeros((voxels, 2 * FACE), np.float32)
    for z in range(EDGE):
        for y in range(EDGE):
            pick[z * FACE + y * EDGE, z * EDGE + y] = 1
            pick[z * FACE + y * EDGE + EDGE - 1, FACE + z * EDGE + y] = 1
    spread = np.zeros((EDGE // 2, 2 * LANES, 2 * LANES), np.float32)
    pack = np.zeros((2 * LANES, LANES), np.float32)
    for half in range(2):
        base = half * LANES
        for y in range(EDGE):
            rows = [y] + ([-1] if y == EDGE - 1 else []) + ([EDGE] if y == 0 else [])
            for x in range(EDGE):
                lane = half * FACE + y * EDGE + x
                pack[base + point(y, x), lane] = 1
                for row in rows:
                    spread[:, lane, base + point(row, x)] = 1
            for pair in range(EDGE // 2):
                z = 2 * pair + half
                for row in rows:
                    spread[pair, LANES + z * EDGE + y, base + point(row, -1)] = 1
                    spread[pair, LANES + FACE + z * EDGE + y, base + point(row, EDGE)] = 1
    to_voxel = np.zeros((words, voxels), np.float32)
    to_voxel[np.arange(voxels) // BITS, np.arange(voxels)] = 1
    region = np.zeros((27, 3 * LANES), np.float32)
    inside = np.zeros((1, LANES), np.float32)
    for y in range(-1, EDGE + 1):
        for x in range(-1, EDGE + 1):
            c = 0 if y < 0 else (2 if y == EDGE else 1)
            e = 0 if x < 0 else (2 if x == EDGE else 1)
            for a in range(3):
                region[9 * a + 3 * c + e, a * LANES + point(y, x)] = 1
            if c == 1 and e == 1:
                inside[0, point(y, x)] = 1
    return pick, spread, pack, to_voxel, region, inside


def kernel(
    n_slab, n_brick, scale, count, *refs,
):
    sources, refs = refs[:count], refs[count:]
    (output_hbm, grad_input_hbm, grad_weight_hbm), held, refs = refs[:3], refs[3 : 3 + count], refs[3 + count :]
    (
        features, cotangent, occupancy, pick, to_voxel, weight, unit, neighbours, region, spread, inside, pack,
    ) = held
    (
    cube, faces, arrived, planes, patches_in, patches_grad, interior, forward, backward,
    part, landed, reduced, across, final, total,
    x_send, x_recv, z_send, z_recv, rs_send, rs_recv, b_send, b_recv, ag_send, ag_recv, in_sems,
    output, grad_input, grad_weight, out_sems,
    ) = refs
    loads = [pltpu.make_async_copy(sources[i], held[i], in_sems.at[i]) for i in range(count)]
    for load in loads:
        load.start()
    slots, channels, voxels = features.shape
    s = lax.axis_index("slab")
    t = lax.axis_index("brick")
    per_row = GROUP // n_slab
    blocks = n_brick // per_row
    column = lax.rem(t, per_row)
    block = t // per_row
    member = s * per_row + column

    def group_device(i):
        other = lax.rem(member + i, GROUP)
        return other, (other // per_row, block * per_row + lax.rem(other, per_row))

    def block_device(i):
        return (s, lax.rem(block + i, blocks) * per_row + column)

    has_left, has_right = t > 0, t < n_brick - 1
    has_below, has_above = s > 0, s < n_slab - 1
    sides = (
        (has_left, (s, t - 1)),
        (has_right, (s, t + 1)),
        (has_below, (s - 1, t)),
        (has_above, (s + 1, t)),
    )
    barrier = pltpu.get_barrier_semaphore()
    for there, device in sides:
        @pl.when(there)
        def _():
            pl.semaphore_signal(barrier, inc=1, device_id=device, device_id_type=MESH)
    for i in range(1, GROUP):
        pl.semaphore_signal(barrier, inc=1, device_id=group_device(i)[1], device_id_type=MESH)
    for i in range(1, blocks):
        pl.semaphore_signal(barrier, inc=1, device_id=block_device(i), device_id_type=MESH)

    for load in loads[:5]:
        load.wait()
    packed = occupancy[...]
    words = jnp.zeros((slots, voxels), jnp.int32)
    for shift in (0, 8, 16):
        byte = jnp.bitwise_and(jnp.right_shift(packed, shift), 255).astype(F32)
        spread_byte = jnp.dot(byte, to_voxel[...], preferred_element_type=F32)
        words = words + jnp.left_shift(spread_byte.astype(jnp.int32), shift)
    place = lax.rem(lax.broadcasted_iota(jnp.int32, (slots, voxels), 1), BITS)
    occupied = jnp.bitwise_and(jnp.right_shift(words, place), 1).astype(F32).astype(BF16)
    ends = []
    for j in range(slots):
        cube[j, :channels, :] = features[j] * occupied[j : j + 1, :]
        cube[j, channels:, :] = cotangent[j] * occupied[j : j + 1, :]
        ends.append(jnp.dot(cube[j], pick[...], preferred_element_type=F32).astype(BF16))
    faces[0] = jnp.concatenate([end[:, :FACE] for end in ends], 1)
    faces[1] = jnp.concatenate([end[:, FACE:] for end in ends], 1)

    beside = (t + n_brick - 1) // n_brick + (2 * n_brick - 2 - t) // n_brick
    upright = (s + n_slab - 1) // n_slab + (2 * n_slab - 2 - s) // n_slab
    pl.semaphore_wait(barrier, GROUP - 1 + blocks - 1 + beside + upright)

    to_left = pltpu.make_async_remote_copy(
        src_ref=faces.at[0], dst_ref=arrived.at[1], send_sem=x_send.at[0], recv_sem=x_recv.at[1],
        device_id=(s, t - 1), device_id_type=MESH)
    to_right = pltpu.make_async_remote_copy(
        src_ref=faces.at[1], dst_ref=arrived.at[0], send_sem=x_send.at[1], recv_sem=x_recv.at[0],
        device_id=(s, t + 1), device_id_type=MESH)

    @pl.when(has_left)
    def _():
        to_left.start()

    @pl.when(has_right)
    def _():
        to_right.start()

    for load in loads[5:]:
        load.wait()
    for k in range(27):
        a, ce = k // 9, k % 9
        forward[a * channels : (a + 1) * channels, ce * channels : (ce + 1) * channels] = weight[k]
    turned = lax.dot_general(
        unit[...], weight[...].reshape(27 * channels, channels), (((1,), (1,)), ((), ())),
        preferred_element_type=F32).astype(BF16)
    for a in range(3):
        backward[a * channels : (a + 1) * channels, :] = turned[:, a * 9 * channels : (a + 1) * 9 * channels]
    present = jnp.where(neighbours[...] >= 0, 1.0, 0.0).astype(F32)
    masks = jnp.dot(present, region[...], preferred_element_type=F32).astype(BF16)

    @pl.when(jnp.logical_not(has_left))
    def _():
        arrived[0] = jnp.zeros(arrived.shape[1:], BF16)

    @pl.when(jnp.logical_not(has_right))
    def _():
        arrived[1] = jnp.zeros(arrived.shape[1:], BF16)

    @pl.when(jnp.logical_not(has_below))
    def _():
        planes[0] = jnp.zeros(planes.shape[1:], BF16)

    @pl.when(jnp.logical_not(has_above))
    def _():
        planes[slots * EDGE + 1] = jnp.zeros(planes.shape[1:], BF16)

    @pl.when(has_right)
    def _():
        to_left.wait_recv()

    @pl.when(has_left)
    def _():
        to_right.wait_recv()

    def spread_pair(j, pair):
        beside = jnp.concatenate(
            [arrived[0][:, j * FACE : (j + 1) * FACE], arrived[1][:, j * FACE : (j + 1) * FACE]], 1)
        both = jnp.concatenate([cube[j, :, pair * LANES : (pair + 1) * LANES], beside], 1)
        wide = jnp.dot(both, spread[pair], preferred_element_type=F32).astype(BF16)
        planes[1 + j * EDGE + 2 * pair] = wide[:, :LANES]
        planes[2 + j * EDGE + 2 * pair] = wide[:, LANES:]

    to_above = pltpu.make_async_remote_copy(
        src_ref=planes.at[slots * EDGE], dst_ref=planes.at[0], send_sem=z_send.at[0], recv_sem=z_recv.at[0],
        device_id=(s + 1, t), device_id_type=MESH)
    to_below = pltpu.make_async_remote_copy(
        src_ref=planes.at[1], dst_ref=planes.at[slots * EDGE + 1], send_sem=z_send.at[1], recv_sem=z_recv.at[1],
        device_id=(s - 1, t), device_id_type=MESH)
    spread_pair(slots - 1, EDGE // 2 - 1)

    @pl.when(has_above)
    def _():
        to_above.start()

    spread_pair(0, 0)

    @pl.when(has_below)
    def _():
        to_below.start()

    for j in range(slots):
        for pair in range(EDGE // 2):
            if (j, pair) not in ((0, 0), (slots - 1, EDGE // 2 - 1)):
                spread_pair(j, pair)

    def make_patches(j, layer):
        kind = 0 if layer == 0 else (2 if layer == EDGE + 1 else 1)
        plane = planes[j * EDGE + layer] * masks[j : j + 1, kind * LANES : (kind + 1) * LANES]
        lanes = slice(layer * LANES, (layer + 1) * LANES)
        top = plane[:channels].astype(F32)
        for ce in range(9):
            step = PITCH * (ce // 3 - 1) + (ce % 3 - 1)
            rows = slice(ce * channels, (ce + 1) * channels)
            moved = top if step == 0 else pltpu.roll(top, (-step) % LANES, 1)
            patches_in[j, rows, lanes] = moved.astype(BF16)
        if kind == 1:
            interior[j, :, (layer - 1) * LANES : layer * LANES] = plane[channels:] * inside[...]

    for j in range(slots):
        for layer in range(EDGE + 2):
            if (j, layer) not in ((0, 0), (slots - 1, EDGE + 1)):
                make_patches(j, layer)

    span = EDGE * LANES
    scatters = [[], [], []]

    def scatter(a):
        terms = None
        for j in range(slots):
            term = lax.dot_general(
                interior[j], patches_in[j, :, a * LANES : a * LANES + span], (((1,), (1,)), ((), ())),
                preferred_element_type=F32)
            terms = term if terms is None else terms + term
        part[a] = terms.reshape(part.shape[1:])
        for i in range(1, GROUP):
            other, device = group_device(i)
            copy = pltpu.make_async_remote_copy(
                src_ref=part.at[a, other], dst_ref=landed.at[a, i - 1],
                send_sem=rs_send.at[a, i - 1], recv_sem=rs_recv.at[a, i - 1], device_id=device, device_id_type=MESH)
            copy.start()
            scatters[a].append(copy)

    scatter(1)

    @pl.when(has_below)
    def _():
        to_above.wait_recv()

    make_patches(0, 0)
    scatter(0)

    @pl.when(has_above)
    def _():
        to_below.wait_recv()

    make_patches(slots - 1, EDGE + 1)
    scatter(2)

    stores = []

    def make_grad_patches(j, layer):
        kind = 0 if layer == 0 else (2 if layer == EDGE + 1 else 1)
        plane = planes[j * EDGE + layer, channels:, :] * masks[j : j + 1, kind * LANES : (kind + 1) * LANES]
        lanes = slice(layer * LANES, (layer + 1) * LANES)
        bottom = plane.astype(F32)
        for ce in range(9):
            step = PITCH * (ce // 3 - 1) + (ce % 3 - 1)
            moved = bottom if step == 0 else pltpu.roll(bottom, step % LANES, 1)
            patches_grad[j, ce * channels : (ce + 1) * channels, lanes] = moved.astype(BF16)

    for j in range(slots):
        for layer in range(EDGE + 2):
            make_grad_patches(j, layer)

    def convolve(j):
        wide = jnp.dot(forward[...], patches_in[j], preferred_element_type=F32)
        rows = [wide[a * channels : (a + 1) * channels, a * LANES : a * LANES + span] for a in range(3)]
        ahead = (rows[0] + rows[1] + rows[2]).astype(BF16)
        wide = jnp.dot(backward[...], patches_grad[j], preferred_element_type=F32)
        rows = [wide[a * channels : (a + 1) * channels, (2 - a) * LANES : (2 - a) * LANES + span] for a in range(3)]
        back = (rows[0] + rows[1] + rows[2]).astype(BF16)
        both = jnp.concatenate([ahead, back], 0)
        for pair in range(EDGE // 2):
            lanes = slice(pair * LANES, (pair + 1) * LANES)
            close = jnp.dot(
                both[:, 2 * pair * LANES : 2 * (pair + 1) * LANES], pack[...], preferred_element_type=F32)
            close = close.astype(BF16) * occupied[j : j + 1, lanes]
            output[j, :, lanes] = close[:channels]
            grad_input[j, :, lanes] = close[channels:]
        for i, (held_out, result) in enumerate(((output, output_hbm), (grad_input, grad_input_hbm))):
            copy = pltpu.make_async_copy(held_out.at[j], result.at[j], out_sems.at[3 + 2 * j + i])
            copy.start()
            stores.append(copy)

    convolve(0)
    exchanges = [[], [], []]
    for a in ORDER:
        mine = part[a, member]
        for copy in scatters[a]:
            copy.wait_recv()
        for i in range(GROUP - 1):
            mine = mine + landed[a, i]
        reduced[a] = mine
        for i in range(1, blocks):
            copy = pltpu.make_async_remote_copy(
                src_ref=reduced.at[a], dst_ref=across.at[a, i - 1],
                send_sem=b_send.at[a, i - 1], recv_sem=b_recv.at[a, i - 1],
                device_id=block_device(i), device_id_type=MESH)
            copy.start()
            exchanges[a].append(copy)
    for j in range(1, slots):
        convolve(j)
    gathers = [[], [], []]
    for a in ORDER:
        whole = reduced[a]
        for copy in exchanges[a]:
            copy.wait_recv()
        for i in range(blocks - 1):
            whole = whole + across[a, i]
        whole = whole * scale
        final[a] = whole
        for i in range(1, GROUP):
            copy = pltpu.make_async_remote_copy(
                src_ref=final.at[a], dst_ref=total.at[a, member],
                send_sem=ag_send.at[a, i - 1], recv_sem=ag_recv.at[a, i - 1],
                device_id=group_device(i)[1], device_id_type=MESH)
            copy.start()
            gathers[a].append(copy)
        total[a, member] = whole

    @pl.when(has_left)
    def _():
        to_left.wait_send()

    @pl.when(has_right)
    def _():
        to_right.wait_send()

    @pl.when(has_above)
    def _():
        to_above.wait_send()

    @pl.when(has_below)
    def _():
        to_below.wait_send()

    for a in ORDER:
        for copy in scatters[a] + exchanges[a]:
            copy.wait_send()
    for a in ORDER:
        for copy in gathers[a]:
            copy.wait()
        rows = total[a].reshape(channels, 9 * channels)
        for ce in range(9):
            grad_weight[9 * a + ce] = rows[:, ce * channels : (ce + 1) * channels]
        taps = pl.ds(9 * a, 9)
        copy = pltpu.make_async_copy(grad_weight.at[taps], grad_weight_hbm.at[taps], out_sems.at[a])
        copy.start()
        stores.append(copy)
    for copy in stores:
        copy.wait()


def place(*refs):
    count = 3
    sources, results, held = refs[:count], refs[count : 2 * count], refs[2 * count : 3 * count]
    load_sems, store_sems = refs[3 * count :]
    loads, stores = [], []
    for i in range(count):
        rows = sources[i].shape[0]
        pieces = 3 if rows % 3 == 0 else 1
        for piece in range(pieces):
            part = pl.ds(piece * (rows // pieces), rows // pieces)
            loads.append(pltpu.make_async_copy(sources[i].at[part], held[i].at[part], load_sems.at[i, piece]))
            stores.append(pltpu.make_async_copy(held[i].at[part], results[i].at[part], store_sems.at[i, piece]))
    for load in loads:
        load.start()
    for load, store in zip(loads, stores):
        load.wait()
        store.start()
    for store in stores:
        store.wait()


def solution(mesh):
    n_slab, n_brick = mesh.shape["slab"], mesh.shape["brick"]

    def per_device(features, weight, cotangent, occupancy, neighbours):
        slots, channels, voxels = features.shape
        pick, spread, pack, to_voxel, region, inside = tables(occupancy.shape[1], voxels)
        sources = (
            features, cotangent, occupancy, jnp.asarray(pick, BF16), jnp.asarray(to_voxel, F32),
            weight, jnp.asarray(np.eye(channels), BF16), neighbours, jnp.asarray(region, F32),
            jnp.asarray(spread, BF16), jnp.asarray(inside, BF16), jnp.asarray(pack, BF16),
        )
        count = len(sources)
        scale = 1.0 / math.sqrt(voxels * slots * n_slab * n_brick)
        blocks = n_brick * n_slab // GROUP
        wide = 2 * channels
        share = (channels // GROUP, 9 * channels)
        padded = (EDGE + 2) * LANES
        dma = pltpu.SemaphoreType.DMA
        results = pl.pallas_call(
            functools.partial(kernel, n_slab, n_brick, scale, count),
            out_shape=(
                jax.ShapeDtypeStruct(features.shape, BF16),
                jax.ShapeDtypeStruct(features.shape, BF16),
                jax.ShapeDtypeStruct(weight.shape, F32),
            ),
            in_specs=[pl.BlockSpec(memory_space=pltpu.HBM)] * count,
            out_specs=[pl.BlockSpec(memory_space=pltpu.HBM)] * 3,
            scratch_shapes=[pltpu.VMEM(source.shape, source.dtype) for source in sources] + [
                pltpu.VMEM((slots, wide, voxels), BF16),
                pltpu.VMEM((2, wide, slots * FACE), BF16),
                pltpu.VMEM((2, wide, slots * FACE), BF16),
                pltpu.VMEM((slots * EDGE + 2, wide, LANES), BF16),
                pltpu.VMEM((slots, 9 * channels, padded), BF16),
                pltpu.VMEM((slots, 9 * channels, padded), BF16),
                pltpu.VMEM((slots, channels, EDGE * LANES), BF16),
                pltpu.VMEM((3 * channels, 9 * channels), BF16),
                pltpu.VMEM((3 * channels, 9 * channels), BF16),
                pltpu.VMEM((3, GROUP) + share, F32),
                pltpu.VMEM((3, GROUP - 1) + share, F32),
                pltpu.VMEM((3,) + share, F32),
                pltpu.VMEM((3, blocks - 1) + share, F32),
                pltpu.VMEM((3,) + share, F32),
                pltpu.VMEM((3, GROUP) + share, F32),
                dma((2,)), dma((2,)), dma((2,)), dma((2,)),
                dma((3, GROUP - 1)), dma((3, GROUP - 1)),
                dma((3, blocks - 1)), dma((3, blocks - 1)),
                dma((3, GROUP - 1)), dma((3, GROUP - 1)), dma((count,)),
                pltpu.VMEM(features.shape, BF16), pltpu.VMEM(features.shape, BF16), pltpu.VMEM(weight.shape, F32),
                dma((3 + 2 * slots,)),
            ],
            compiler_params=pltpu.CompilerParams(
                collective_id=0, has_side_effects=True, vmem_limit_bytes=63 * 1024 * 1024
            ),
        )(*sources)
        return pl.pallas_call(
            place,
            out_shape=tuple(jax.ShapeDtypeStruct(result.shape, result.dtype) for result in results),
            in_specs=[pl.BlockSpec(memory_space=pltpu.HBM)] * 3,
            out_specs=[pl.BlockSpec(memory_space=pltpu.HBM)] * 3,
            scratch_shapes=[pltpu.VMEM(result.shape, result.dtype) for result in results] + [dma((3, 3)), dma((3, 3))],
            compiler_params=pltpu.CompilerParams(vmem_limit_bytes=63 * 1024 * 1024),
        )(*results)

    placed = (
        P(("slab", "brick"), None, None),
        P(),
        P(("slab", "brick"), None, None),
        P(("slab", "brick"), None),
        P(("slab", "brick"), None),
    )
    return jax.shard_map(
        per_device,
        mesh=mesh,
        in_specs=placed,
        out_specs=(P(("slab", "brick"), None, None), P(("slab", "brick"), None, None), P()),
        check_vma=False,
    )
```
